32 devices in a mesh: seq: 8 (over z, x), feat: 4 (over y, core).
Axes of the slice: x: 2, y: 2, z: 4, core: 2. Of those that a mesh axis runs over, the one named last changes fastest.
Arguments:
- tokens: bfloat16 [8192, 4096], P('seq', 'feat'), may hold values from -18 to 18
- segment_ids: int32 [8192], P('seq'), may hold values from 0 to 5, never falling along the last dimension, each value on 1 to 4096 neighbouring positions
- q_weight: bfloat16 [4096, 4096], P('seq', 'feat'), may hold values from -0.09375 to 0.09375
- k_weight: bfloat16 [4096, 1024], P('seq'), may hold values from -0.09375 to 0.09375
- v_weight: bfloat16 [4096, 1024], P('seq'), may hold values from -0.09375 to 0.09375
- o_weight: bfloat16 [4096, 4096], P('seq', 'feat'), may hold values from -0.09375 to 0.09375
Outputs:
- attention_out: bfloat16 [8192, 4096], P('seq', 'feat')
The draws below stay inside these ranges and needn't reach their ends.
Inputs may be any that keep to these rules, and one draw needn't show every extreme that they name: `segment_ids`: document numbers never fall along the window; each document is 1 to 4096 positions long and one is exactly that long.
All inputs are finite; a program needn't handle non-finite values.
Results may differ from the reference program's by a relative error of at most 0.011.
Values may be sent and summed in bfloat16 or wider, within the bound.
A program may use at most 192 MiB of HBM per device.

```python
import math
import jax
import jax.numpy as jnp
import numpy as np
from jax import lax

H = 32
KVH = 8
HD = 128
D = 4096
KVD = 1024
DOCS = 6
TOKENS = 8192


def draw_tokens(key, part):
    key = jax.random.fold_in(key, 7)
    first = jax.random.fold_in(key, 0)
    return jnp.clip(jax.random.normal(first, (TOKENS, D), jnp.float32), -6.0, 6.0).astype(jnp.bfloat16)


def levels(stream_key, extent, cuts, least, high):
    gain = 1.0
    for axis_at, parts in cuts:
        heights = jax.random.uniform(jax.random.fold_in(jax.random.fold_in(stream_key, 6), axis_at), (parts,), jnp.float32, least / len(cuts), high / len(cuts))
        gain = gain * jnp.repeat(jnp.exp(heights), extent[axis_at] // parts).reshape((-1,) + (1,) * (len(extent) - 1 - axis_at))
    return gain


def profile(count, total, bound, slope):
    loads = [(1 << 20) // math.isqrt(standing ** slope) + 1 for standing in range(2, count + 1)]
    rest, counts = total - bound - (count - 1), [1] * (count - 1)
    while rest > 0:
        free = [i for i in range(count - 1) if counts[i] < bound]
        mass, budget = sum([loads[i] for i in free]), rest
        for i in free:
            extra = min(bound - counts[i], max(1, budget * loads[i] // mass), rest)
            counts[i] = counts[i] + extra
            rest = rest - extra
    return np.array([bound] + counts)


def uneven_parts(stream_key, number_of, total, limit, lean):
    if number_of == 2:
        one = jax.random.randint(stream_key, (), max(1, total - limit), min(limit, total - 1) + 1)
        return jnp.stack([one, total - one])
    lengths = jnp.asarray(profile(number_of, total, limit, lean), jnp.int32)
    couples = (number_of - 1) // 2
    giver, sink = lengths[1:1 + 2 * couples:2], lengths[2:2 + 2 * couples:2]
    room = jnp.minimum(giver - 1, limit - sink)
    passed = jax.random.randint(jax.random.fold_in(stream_key, 1), (couples,), 0, 1 << 20) % (room + 1)
    lengths = lengths.at[1:1 + 2 * couples:2].set(giver - passed).at[2:2 + 2 * couples:2].set(sink + passed)
    return lengths[jax.random.permutation(jax.random.fold_in(stream_key, 2), number_of)]


def gaussian(own_key, dims, deviation, most, cuts=(), kind=jnp.bfloat16):
    entries = jax.random.normal(own_key, dims, jnp.float32) * deviation
    if len(cuts) > 0:
        entries = levels(own_key, dims, cuts, -0.22, 0.18) * entries
    return jnp.clip(entries, min=-most, max=most).astype(kind)


def setup_inputs(seed: int = 0) -> dict:
    arg_keys = jax.random.split(jax.random.key(seed), 7)
    return {
        "tokens": draw_tokens(jax.random.fold_in(arg_keys[6], 71), 0),
        "segment_ids": jnp.searchsorted(jnp.cumsum(uneven_parts(arg_keys[1], DOCS, TOKENS, TOKENS // 2, 0)), jnp.arange(TOKENS), side="right").astype(jnp.int32),
        "q_weight": gaussian(arg_keys[2], (D, D), D ** -0.5, 0.09375, ((0, 8), (1, 4))),
        "k_weight": gaussian(arg_keys[3], (D, KVD), D ** -0.5, 0.09375, ((0, 8),)),
        "v_weight": gaussian(arg_keys[4], (D, KVD), D ** -0.5, 0.09375, ((0, 8),)),
        "o_weight": gaussian(arg_keys[5], (D, D), D ** -0.5, 0.09375, ((0, 8), (1, 4))),
    }


rope_base = 500000.0

def rotary(matrix, positions):
    columns = matrix.shape[1]
    pair_index = (jnp.arange(columns // 2, dtype=jnp.int32) % (HD // 2)).astype(jnp.float32)
    frequency = jnp.exp(-(2.0 * pair_index / HD) * math.log(rope_base))
    angle = positions.astype(jnp.float32)[:, None] * frequency[None, :]
    cosine = jnp.cos(angle)
    sine = jnp.sin(angle)
    paired = matrix.reshape(matrix.shape[0], columns // 2, 2)
    first = paired[..., 0]
    second = paired[..., 1]
    turned = jnp.stack([first * cosine - second * sine, first * sine + second * cosine], -1)
    return turned.reshape(matrix.shape)

def reference(tokens, segment_ids, q_weight, k_weight, v_weight, o_weight):
    positions = jnp.arange(TOKENS, dtype=jnp.int32)
    queries = rotary(jnp.dot(tokens, q_weight, preferred_element_type=jnp.float32), positions).astype(jnp.bfloat16)
    keys = rotary(jnp.dot(tokens, k_weight, preferred_element_type=jnp.float32), positions).astype(jnp.bfloat16)
    values = jnp.dot(tokens, v_weight, preferred_element_type=jnp.float32).astype(jnp.bfloat16)
    group = H // KVH
    block_rows = min(TOKENS, 1024)
    blocks = TOKENS // block_rows
    score_scale = 1.0 / math.sqrt(HD)
    key_positions = jnp.arange(TOKENS, dtype=jnp.int32)

    def one_block(number):
        head = (number // blocks).astype(jnp.int32)
        start = (number % blocks * block_rows).astype(jnp.int32)
        zero = jnp.zeros((), jnp.int32)
        query_block = lax.dynamic_slice(queries, (start, head * HD), (block_rows, HD))
        key_head = (head // group).astype(jnp.int32)
        key_block = lax.dynamic_slice(keys, (zero, key_head * HD), (TOKENS, HD))
        value_block = lax.dynamic_slice(values, (zero, key_head * HD), (TOKENS, HD))
        scores = jnp.dot(query_block, key_block.T, preferred_element_type=jnp.float32) * score_scale
        query_positions = start + jnp.arange(block_rows, dtype=jnp.int32)
        query_segments = lax.dynamic_slice(segment_ids, (start,), (block_rows,))
        allowed = (key_positions[None, :] <= query_positions[:, None]) & (segment_ids[None, :] == query_segments[:, None])
        scores = jnp.where(allowed, scores, -1e+30)
        highest = lax.optimization_barrier(jnp.max(scores, axis=-1, keepdims=True))
        probs = jnp.where(allowed, jnp.exp(scores - highest), 0.0)
        total = lax.optimization_barrier(jnp.sum(probs, axis=-1, keepdims=True))
        mixed = jnp.dot(probs.astype(jnp.bfloat16), value_block, preferred_element_type=jnp.float32) / total
        return mixed.astype(jnp.bfloat16)
    pieces = lax.map(one_block, jnp.arange(H * blocks, dtype=jnp.int32))
    attended = pieces.reshape(H, blocks, block_rows, HD).transpose(1, 2, 0, 3).reshape(TOKENS, D)
    return jnp.dot(attended, o_weight, preferred_element_type=jnp.float32).astype(jnp.bfloat16)
```

```python
import functools
import math

import jax
import jax.numpy as jnp
from jax import lax
from jax.experimental import pallas as pl
from jax.experimental.pallas import tpu as pltpu
from jax.sharding import PartitionSpec as P

H = 32
KVH = 8
HD = 128
KVD = 1024
rope_base = 500000.0
VMEM_BYTES = 48 * 1024 * 1024
ROWS = 256
KEYS = 512


def rope_tables(positions):
    lane = jnp.arange(HD, dtype=jnp.int32)
    pair_index = (lane // 2).astype(jnp.float32)
    frequency = jnp.exp(-(2.0 * pair_index / HD) * math.log(rope_base))
    angle = positions.astype(jnp.float32)[:, None] * frequency[None, :]
    sign = jnp.where(lane % 2 == 0, -1.0, 1.0)
    return jnp.cos(angle), jnp.sin(angle) * sign[None, :]


def project_kernel(rope_tiles, x_ref, w_ref, cos_ref, sin_ref, o_ref):
    column = pl.program_id(0)
    rows = x_ref.shape[0]

    @pl.loop(0, rows // ROWS)
    def _(step):
        at = pl.ds(pl.multiple_of(step * ROWS, ROWS), ROWS)
        raw = jnp.dot(x_ref[at, :], w_ref[...], preferred_element_type=jnp.float32)

        def turned():
            cosine = cos_ref[at, :]
            sine = sin_ref[at, :]
            even = lax.broadcasted_iota(jnp.int32, (ROWS, HD), 1) % 2 == 0
            for head in range(w_ref.shape[1] // HD):
                part = raw[:, head * HD : (head + 1) * HD]
                other = jnp.where(
                    even, pltpu.roll(part, HD - 1, 1), pltpu.roll(part, 1, 1)
                )
                o_ref[at, head * HD : (head + 1) * HD] = (
                    part * cosine + other * sine
                ).astype(o_ref.dtype)

        def plain():
            o_ref[at, :] = raw.astype(o_ref.dtype)

        if rope_tiles is None:
            turned()
        else:
            pl.when(column < rope_tiles)(turned)
            pl.when(column >= rope_tiles)(plain)


def project(x, w, tables, tile, rope_tiles):
    rows, depth = x.shape
    columns = w.shape[1]
    return pl.pallas_call(
        functools.partial(project_kernel, rope_tiles),
        grid=(columns // tile,),
        out_shape=jax.ShapeDtypeStruct((rows, columns), jnp.bfloat16),
        in_specs=[
            pl.BlockSpec((rows, depth), lambda j: (0, 0)),
            pl.BlockSpec((depth, tile), lambda j: (0, j)),
            pl.BlockSpec((rows, HD), lambda j: (0, 0)),
            pl.BlockSpec((rows, HD), lambda j: (0, 0)),
        ],
        out_specs=pl.BlockSpec((rows, tile), lambda j: (0, j)),
        compiler_params=pltpu.CompilerParams(vmem_limit_bytes=VMEM_BYTES),
        cost_estimate=pl.CostEstimate(
            flops=2 * rows * depth * columns,
            bytes_accessed=2 * (rows * depth + depth * columns + rows * columns),
            transcendentals=0,
        ),
    )(x, w, *tables)


def attend_kernel(bounds, q_ref, k_ref, v_ref, start_ref, o_ref, m_ref, acc_ref):
    tile = pl.program_id(1)
    heads = q_ref.shape[1] // HD
    begin = bounds[0] + tile * ROWS
    first_start = bounds[1 + 2 * tile]
    last_start = bounds[2 + 2 * tile]
    low = first_start // KEYS
    high = (begin + ROWS - 1) // KEYS + 1
    full_low = jnp.minimum((last_start + KEYS - 1) // KEYS, high)
    full_high = jnp.clip((begin + 1) // KEYS, full_low, high)
    m_ref[...] = jnp.full(m_ref.shape, -1e30, jnp.float32)
    acc_ref[...] = jnp.zeros(acc_ref.shape, jnp.float32)
    ones = jnp.ones((KEYS, HD), jnp.bfloat16)

    def block(number, masked):
        at = pl.ds(pl.multiple_of(number * KEYS, KEYS), KEYS)
        keys = k_ref[at, :]
        values = jnp.concatenate([v_ref[at, :], ones], axis=1)
        if masked:
            key_at = number * KEYS + lax.broadcasted_iota(jnp.int32, (ROWS, KEYS), 1)
            query_at = begin + lax.broadcasted_iota(jnp.int32, (ROWS, KEYS), 0)
            allowed = (key_at <= query_at) & (key_at >= start_ref[...])
        for head in range(heads):
            scores = lax.dot_general(
                q_ref[:, head * HD : (head + 1) * HD],
                keys,
                (((1,), (1,)), ((), ())),
                preferred_element_type=jnp.float32,
            )
            if masked:
                scores = jnp.where(allowed, scores, -1e30)
            before = m_ref[head]
            after = jnp.maximum(before, jnp.max(scores, axis=1, keepdims=True))
            m_ref[head] = after
            probs = jnp.exp2(scores - jnp.concatenate([after] * (KEYS // HD), axis=1))
            rescale = jnp.exp2(before - after)
            acc_ref[head] = acc_ref[head] * jnp.concatenate(
                [rescale, rescale], axis=1
            ) + jnp.dot(
                probs.astype(jnp.bfloat16), values, preferred_element_type=jnp.float32
            )

    pl.loop(low, full_low)(lambda number: block(number, True))
    pl.loop(full_low, full_high)(lambda number: block(number, False))
    pl.loop(full_high, high)(lambda number: block(number, True))
    for head in range(heads):
        o_ref[:, head * HD : (head + 1) * HD] = (
            acc_ref[head, :, :HD] / acc_ref[head, :, HD:]
        ).astype(o_ref.dtype)


def attend(queries, kv, starts, query_start, kv_heads):
    rows, columns = queries.shape
    total = kv.shape[0]
    group = columns // HD // kv_heads
    tiles = rows // ROWS
    ends = jnp.stack([starts[::ROWS], starts[ROWS - 1 :: ROWS]], axis=1).reshape(-1)
    bounds = jnp.concatenate([query_start[None], ends]).astype(jnp.int32)
    return pl.pallas_call(
        attend_kernel,
        grid_spec=pltpu.PrefetchScalarGridSpec(
            num_scalar_prefetch=1,
            grid=(kv_heads, tiles),
            in_specs=[
                pl.BlockSpec((ROWS, group * HD), lambda h, t, b: (t, h)),
                pl.BlockSpec((total, HD), lambda h, t, b: (0, h)),
                pl.BlockSpec((total, HD), lambda h, t, b: (0, kv_heads + h)),
                pl.BlockSpec((ROWS, 1), lambda h, t, b: (t, 0)),
            ],
            out_specs=pl.BlockSpec((ROWS, group * HD), lambda h, t, b: (t, h)),
            scratch_shapes=[
                pltpu.VMEM((group, ROWS, HD), jnp.float32),
                pltpu.VMEM((group, ROWS, 2 * HD), jnp.float32),
            ],
        ),
        out_shape=jax.ShapeDtypeStruct((rows, columns), jnp.bfloat16),
        compiler_params=pltpu.CompilerParams(vmem_limit_bytes=VMEM_BYTES),
        cost_estimate=pl.CostEstimate(
            flops=2 * rows * columns * total,
            bytes_accessed=2 * (2 * rows * columns + 2 * total * kv_heads * HD),
            transcendentals=rows * columns // HD * total // 2,
        ),
    )(bounds, queries, kv, kv, starts[:, None])


def local(tokens, segment_ids, q_weight, k_weight, v_weight, o_weight):
    feat_count = lax.axis_size("feat")
    feat_index = lax.axis_index("feat")
    head_count = q_weight.shape[1] // HD
    group = H // KVH
    kv_width = max(KVD // feat_count, HD)
    kv_heads = kv_width // HD
    kv_start = feat_index * head_count // group * HD
    query_count = tokens.shape[0]
    query_start = lax.axis_index("seq") * query_count
    positions = query_start + jnp.arange(query_count, dtype=jnp.int32)
    cosine, sine = rope_tables(positions)
    factor = math.log2(math.e) / math.sqrt(HD)

    segments = lax.all_gather(segment_ids, "seq", axis=0, tiled=True)
    starts = jnp.sum(
        segments[None, :] < segment_ids[:, None], axis=1, dtype=jnp.int32
    )
    kv_slice = jnp.concatenate(
        [
            lax.dynamic_slice_in_dim(k_weight, kv_start, kv_width, 1),
            lax.dynamic_slice_in_dim(v_weight, kv_start, kv_width, 1),
        ],
        axis=1,
    )
    piece = lax.all_gather(tokens, "feat", axis=1, tiled=True)
    kv_panel = lax.all_gather(kv_slice, "seq", axis=0, tiled=True)
    kv_local = project(piece, kv_panel, (cosine, sine), kv_width, 1)
    q_panel = lax.all_gather(q_weight, "seq", axis=0, tiled=True)
    kv = lax.all_gather(kv_local, "seq", axis=0, tiled=True)
    queries = project(piece, q_panel, (cosine * factor, sine * factor), 256, None)
    o_panel = lax.all_gather(o_weight, "seq", axis=0, tiled=True)
    attended = attend(queries, kv, starts, query_start, kv_heads)
    result = jnp.dot(
        lax.all_gather(attended, "feat", axis=1, tiled=True),
        o_panel,
        preferred_element_type=jnp.float32,
    )
    return result.astype(jnp.bfloat16)


def solution(mesh):
    in_specs = (
        P("seq", "feat"),
        P("seq"),
        P("seq", "feat"),
        P("seq", None),
        P("seq", None),
        P("seq", "feat"),
    )
    out_specs = P("seq", "feat")
    return jax.shard_map(local, mesh=mesh, in_specs=in_specs, out_specs=out_specs, check_vma=False)
```

```python
import functools
import math

import jax
import jax.numpy as jnp
from jax import lax
from jax.experimental import pallas as pl
from jax.experimental.pallas import tpu as pltpu
from jax.sharding import PartitionSpec as P

H = 32
KVH = 8
HD = 128
KVD = 1024
rope_base = 500000.0
VMEM_BYTES = 48 * 1024 * 1024
ROWS = 256
KEYS = 512


def rope_tables(positions):
    lane = jnp.arange(HD, dtype=jnp.int32)
    pair_index = (lane // 2).astype(jnp.float32)
    frequency = jnp.exp(-(2.0 * pair_index / HD) * math.log(rope_base))
    angle = positions.astype(jnp.float32)[:, None] * frequency[None, :]
    sign = jnp.where(lane % 2 == 0, -1.0, 1.0)
    return jnp.cos(angle), jnp.sin(angle) * sign[None, :]


def project_kernel(rope_tiles, count, offsets, *refs):
    x_refs = refs[:count]
    w_ref, cos_ref, sin_ref, o_ref = refs[count:]
    column = pl.program_id(0)
    rows, depth = x_refs[0].shape

    @pl.loop(0, rows // ROWS)
    def _(step):
        at = pl.ds(pl.multiple_of(step * ROWS, ROWS), ROWS)
        raw = jnp.zeros((ROWS, w_ref.shape[1]), jnp.float32)
        for number in range(count):
            begin = pl.multiple_of(offsets[number], depth)
            raw += jnp.dot(
                x_refs[number][at, :],
                w_ref[pl.ds(begin, depth), :],
                preferred_element_type=jnp.float32,
            )

        def turned():
            cosine = cos_ref[at, :]
            sine = sin_ref[at, :]
            even = lax.broadcasted_iota(jnp.int32, (ROWS, HD), 1) % 2 == 0
            for head in range(w_ref.shape[1] // HD):
                part = raw[:, head * HD : (head + 1) * HD]
                other = jnp.where(
                    even, pltpu.roll(part, HD - 1, 1), pltpu.roll(part, 1, 1)
                )
                o_ref[at, head * HD : (head + 1) * HD] = (
                    part * cosine + other * sine
                ).astype(o_ref.dtype)

        def plain():
            o_ref[at, :] = raw.astype(o_ref.dtype)

        if rope_tiles == "all":
            turned()
        elif rope_tiles == "none":
            plain()
        else:
            pl.when(column < rope_tiles)(turned)
            pl.when(column >= rope_tiles)(plain)


def project(pieces, offsets, w, tables, tile, rope_tiles):
    rows, depth = pieces[0].shape
    total = depth * len(pieces)
    columns = w.shape[1]
    whole = lambda j, o: (0, 0)
    return pl.pallas_call(
        functools.partial(project_kernel, rope_tiles, len(pieces)),
        grid_spec=pltpu.PrefetchScalarGridSpec(
            num_scalar_prefetch=1,
            grid=(columns // tile,),
            in_specs=[pl.BlockSpec((rows, depth), whole)] * len(pieces)
            + [
                pl.BlockSpec((total, tile), lambda j, o: (0, j)),
                pl.BlockSpec((rows, HD), whole),
                pl.BlockSpec((rows, HD), whole),
            ],
            out_specs=pl.BlockSpec((rows, tile), lambda j, o: (0, j)),
        ),
        out_shape=jax.ShapeDtypeStruct((rows, columns), jnp.bfloat16),
        compiler_params=pltpu.CompilerParams(vmem_limit_bytes=VMEM_BYTES),
        cost_estimate=pl.CostEstimate(
            flops=2 * rows * total * columns,
            bytes_accessed=2 * (rows * total + total * columns + rows * columns),
            transcendentals=0,
        ),
    )(offsets, *pieces, w, *tables)


def exchange(block, axis):
    count = lax.axis_size(axis)
    pieces, numbers = [block], [0]
    bit = count // 2
    while bit:
        pairs = [(index, index ^ bit) for index in range(count)]
        pieces = pieces + [lax.ppermute(piece, axis, pairs) for piece in pieces]
        numbers = numbers + [number ^ bit for number in numbers]
        bit //= 2
    return pieces, numbers


def attend_kernel(bounds, q_ref, k_ref, v_ref, start_ref, o_ref, m_ref, acc_ref):
    tile = pl.program_id(1)
    heads = q_ref.shape[1] // HD
    begin = bounds[0] + tile * ROWS
    first_start = bounds[1 + 2 * tile]
    last_start = bounds[2 + 2 * tile]
    low = first_start // KEYS
    high = (begin + ROWS - 1) // KEYS + 1
    full_low = jnp.minimum((last_start + KEYS - 1) // KEYS, high)
    full_high = jnp.clip((begin + 1) // KEYS, full_low, high)
    m_ref[...] = jnp.full(m_ref.shape, -1e30, jnp.float32)
    acc_ref[...] = jnp.zeros(acc_ref.shape, jnp.float32)
    ones = jnp.ones((KEYS, HD), jnp.bfloat16)

    def block(number, masked):
        at = pl.ds(pl.multiple_of(number * KEYS, KEYS), KEYS)
        keys = k_ref[at, :]
        values = jnp.concatenate([v_ref[at, :], ones], axis=1)
        if masked:
            key_at = number * KEYS + lax.broadcasted_iota(jnp.int32, (ROWS, KEYS), 1)
            query_at = begin + lax.broadcasted_iota(jnp.int32, (ROWS, KEYS), 0)
            allowed = (key_at <= query_at) & (key_at >= start_ref[...])
        for head in range(heads):
            scores = lax.dot_general(
                q_ref[:, head * HD : (head + 1) * HD],
                keys,
                (((1,), (1,)), ((), ())),
                preferred_element_type=jnp.float32,
            )
            if masked:
                scores = jnp.where(allowed, scores, -1e30)
            before = m_ref[head]
            after = jnp.maximum(before, jnp.max(scores, axis=1, keepdims=True))
            m_ref[head] = after
            probs = jnp.exp2(scores - jnp.concatenate([after] * (KEYS // HD), axis=1))
            rescale = jnp.exp2(before - after)
            acc_ref[head] = acc_ref[head] * jnp.concatenate(
                [rescale, rescale], axis=1
            ) + jnp.dot(
                probs.astype(jnp.bfloat16), values, preferred_element_type=jnp.float32
            )

    pl.loop(low, full_low)(lambda number: block(number, True))
    pl.loop(full_low, full_high)(lambda number: block(number, False))
    pl.loop(full_high, high)(lambda number: block(number, True))
    for head in range(heads):
        o_ref[:, head * HD : (head + 1) * HD] = (
            acc_ref[head, :, :HD] / acc_ref[head, :, HD:]
        ).astype(o_ref.dtype)


def attend(queries, kv, starts, query_start, kv_heads):
    rows, columns = queries.shape
    total = kv.shape[0]
    group = columns // HD // kv_heads
    tiles = rows // ROWS
    ends = jnp.stack([starts[::ROWS], starts[ROWS - 1 :: ROWS]], axis=1).reshape(-1)
    bounds = jnp.concatenate([query_start[None], ends]).astype(jnp.int32)
    return pl.pallas_call(
        attend_kernel,
        grid_spec=pltpu.PrefetchScalarGridSpec(
            num_scalar_prefetch=1,
            grid=(kv_heads, tiles),
            in_specs=[
                pl.BlockSpec((ROWS, group * HD), lambda h, t, b: (t, h)),
                pl.BlockSpec((total, HD), lambda h, t, b: (0, h)),
                pl.BlockSpec((total, HD), lambda h, t, b: (0, kv_heads + h)),
                pl.BlockSpec((ROWS, 1), lambda h, t, b: (t, 0)),
            ],
            out_specs=pl.BlockSpec((ROWS, group * HD), lambda h, t, b: (t, h)),
            scratch_shapes=[
                pltpu.VMEM((group, ROWS, HD), jnp.float32),
                pltpu.VMEM((group, ROWS, 2 * HD), jnp.float32),
            ],
        ),
        out_shape=jax.ShapeDtypeStruct((rows, columns), jnp.bfloat16),
        compiler_params=pltpu.CompilerParams(vmem_limit_bytes=VMEM_BYTES),
        cost_estimate=pl.CostEstimate(
            flops=2 * rows * columns * total,
            bytes_accessed=2 * (2 * rows * columns + 2 * total * kv_heads * HD),
            transcendentals=rows * columns // HD * total // 2,
        ),
    )(bounds, queries, kv, kv, starts[:, None])


def local(tokens, segment_ids, q_weight, k_weight, v_weight, o_weight):
    feat_count = lax.axis_size("feat")
    feat_index = lax.axis_index("feat")
    head_count = q_weight.shape[1] // HD
    group = H // KVH
    kv_width = max(KVD // feat_count, HD)
    kv_heads = kv_width // HD
    kv_start = feat_index * head_count // group * HD
    query_count = tokens.shape[0]
    query_start = lax.axis_index("seq") * query_count
    positions = query_start + jnp.arange(query_count, dtype=jnp.int32)
    cosine, sine = rope_tables(positions)
    factor = math.log2(math.e) / math.sqrt(HD)

    segments = lax.all_gather(segment_ids, "seq", axis=0, tiled=True)
    starts = jnp.sum(
        segments[None, :] < segment_ids[:, None], axis=1, dtype=jnp.int32
    )
    kv_slice = jnp.concatenate(
        [
            lax.dynamic_slice_in_dim(k_weight, kv_start, kv_width, 1),
            lax.dynamic_slice_in_dim(v_weight, kv_start, kv_width, 1),
        ],
        axis=1,
    )
    pieces, numbers = exchange(tokens, "feat")
    sources = jnp.stack([feat_index ^ number for number in numbers])
    token_rows = sources * tokens.shape[1]
    kv_panel = lax.all_gather(kv_slice, "seq", axis=0, tiled=True)
    kv_local = project(pieces, token_rows, kv_panel, (cosine, sine), kv_width, 1)
    q_panel = lax.all_gather(q_weight, "seq", axis=0, tiled=True)
    kv = lax.all_gather(kv_local, "seq", axis=0, tiled=True)
    queries = project(
        pieces, token_rows, q_panel, (cosine * factor, sine * factor), 256, "all"
    )
    o_panel = lax.all_gather(o_weight, "seq", axis=0, tiled=True)
    attended = attend(queries, kv, starts, query_start, kv_heads)
    mixed, _ = exchange(attended, "feat")
    attended_rows = sources * attended.shape[1]
    return project(mixed, attended_rows, o_panel, (cosine, sine), 256, "none")


def solution(mesh):
    in_specs = (
        P("seq", "feat"),
        P("seq"),
        P("seq", "feat"),
        P("seq", None),
        P("seq", None),
        P("seq", "feat"),
    )
    out_specs = P("seq", "feat")
    return jax.shard_map(local, mesh=mesh, in_specs=in_specs, out_specs=out_specs, check_vma=False)
```

```python
import functools
import math

import jax
import jax.numpy as jnp
from jax import lax
from jax.experimental import pallas as pl
from jax.experimental.pallas import tpu as pltpu
from jax.sharding import PartitionSpec as P

H = 32
KVH = 8
HD = 128
KVD = 1024
rope_base = 500000.0
VMEM_BYTES = 48 * 1024 * 1024
ROWS = 256
KEYS = 512


def rope_tables(positions):
    lane = jnp.arange(HD, dtype=jnp.int32)
    pair_index = (lane // 2).astype(jnp.float32)
    frequency = jnp.exp(-(2.0 * pair_index / HD) * math.log(rope_base))
    angle = positions.astype(jnp.float32)[:, None] * frequency[None, :]
    sign = jnp.where(lane % 2 == 0, -1.0, 1.0)
    return jnp.cos(angle), jnp.sin(angle) * sign[None, :]


def project_kernel(rope_tiles, count, w_count, offsets, w_offsets, *refs):
    x_refs = refs[:count]
    w_refs = refs[count : count + w_count]
    cos_ref, sin_ref, o_ref = refs[count + w_count : count + w_count + 3]
    column = pl.program_id(0)
    rows, depth = x_refs[0].shape
    w_ref = w_refs[0]
    if w_count > 1:
        w_ref = refs[-1]
        part_rows = w_refs[0].shape[0]
        for number in range(w_count):
            begin = pl.multiple_of(w_offsets[number], part_rows)
            w_ref[pl.ds(begin, part_rows), :] = w_refs[number][...]

    @pl.loop(0, rows // ROWS)
    def _(step):
        at = pl.ds(pl.multiple_of(step * ROWS, ROWS), ROWS)
        raw = jnp.zeros((ROWS, w_ref.shape[1]), jnp.float32)
        for number in range(count):
            begin = pl.multiple_of(offsets[number], depth)
            raw += jnp.dot(
                x_refs[number][at, :],
                w_ref[pl.ds(begin, depth), :],
                preferred_element_type=jnp.float32,
            )

        def turned():
            cosine = cos_ref[at, :]
            sine = sin_ref[at, :]
            even = lax.broadcasted_iota(jnp.int32, (ROWS, HD), 1) % 2 == 0
            for head in range(w_ref.shape[1] // HD):
                part = raw[:, head * HD : (head + 1) * HD]
                other = jnp.where(
                    even, pltpu.roll(part, HD - 1, 1), pltpu.roll(part, 1, 1)
                )
                o_ref[at, head * HD : (head + 1) * HD] = (
                    part * cosine + other * sine
                ).astype(o_ref.dtype)

        def plain():
            o_ref[at, :] = raw.astype(o_ref.dtype)

        if rope_tiles == "all":
            turned()
        elif rope_tiles == "none":
            plain()
        else:
            pl.when(column < rope_tiles)(turned)
            pl.when(column >= rope_tiles)(plain)


def project(pieces, offsets, w_pieces, w_offsets, tables, tile, rope_tiles):
    rows, depth = pieces[0].shape
    total = depth * len(pieces)
    columns = w_pieces[0].shape[1]
    whole = lambda j, o, p: (0, 0)
    return pl.pallas_call(
        functools.partial(project_kernel, rope_tiles, len(pieces), len(w_pieces)),
        grid_spec=pltpu.PrefetchScalarGridSpec(
            num_scalar_prefetch=2,
            grid=(columns // tile,),
            in_specs=[pl.BlockSpec((rows, depth), whole)] * len(pieces)
            + [
                pl.BlockSpec((total // len(w_pieces), tile), lambda j, o, p: (0, j))
            ]
            * len(w_pieces)
            + [pl.BlockSpec((rows, HD), whole)] * 2,
            out_specs=pl.BlockSpec((rows, tile), lambda j, o, p: (0, j)),
            scratch_shapes=[pltpu.VMEM((total, tile), jnp.bfloat16)]
            if len(w_pieces) > 1
            else [],
        ),
        out_shape=jax.ShapeDtypeStruct((rows, columns), jnp.bfloat16),
        compiler_params=pltpu.CompilerParams(vmem_limit_bytes=VMEM_BYTES),
        cost_estimate=pl.CostEstimate(
            flops=2 * rows * total * columns,
            bytes_accessed=2 * (rows * total + total * columns + rows * columns),
            transcendentals=0,
        ),
    )(offsets, w_offsets, *pieces, *w_pieces, *tables)


def exchange(block, axis):
    count = lax.axis_size(axis)
    pieces, numbers = [block], [0]
    bit = count // 2
    while bit:
        pairs = [(index, index ^ bit) for index in range(count)]
        pieces = pieces + [lax.ppermute(piece, axis, pairs) for piece in pieces]
        numbers = numbers + [number ^ bit for number in numbers]
        bit //= 2
    return pieces, numbers


def attend_kernel(bounds, q_ref, k_ref, v_ref, start_ref, o_ref, m_ref, acc_ref):
    tile = pl.program_id(1)
    heads = q_ref.shape[1] // HD
    begin = bounds[0] + tile * ROWS
    first_start = bounds[1 + 2 * tile]
    last_start = bounds[2 + 2 * tile]
    low = first_start // KEYS
    high = (begin + ROWS - 1) // KEYS + 1
    full_low = jnp.minimum((last_start + KEYS - 1) // KEYS, high)
    full_high = jnp.clip((begin + 1) // KEYS, full_low, high)
    m_ref[...] = jnp.full(m_ref.shape, -1e30, jnp.float32)
    acc_ref[...] = jnp.zeros(acc_ref.shape, jnp.float32)
    ones = jnp.ones((KEYS, HD), jnp.bfloat16)

    def block(number, masked):
        at = pl.ds(pl.multiple_of(number * KEYS, KEYS), KEYS)
        keys = k_ref[at, :]
        values = jnp.concatenate([v_ref[at, :], ones], axis=1)
        if masked:
            key_at = number * KEYS + lax.broadcasted_iota(jnp.int32, (ROWS, KEYS), 1)
            query_at = begin + lax.broadcasted_iota(jnp.int32, (ROWS, KEYS), 0)
            allowed = (key_at <= query_at) & (key_at >= start_ref[...])
        for head in range(heads):
            scores = lax.dot_general(
                q_ref[:, head * HD : (head + 1) * HD],
                keys,
                (((1,), (1,)), ((), ())),
                preferred_element_type=jnp.float32,
            )
            if masked:
                scores = jnp.where(allowed, scores, -1e30)
            before = m_ref[head]
            after = jnp.maximum(before, jnp.max(scores, axis=1, keepdims=True))
            m_ref[head] = after
            probs = jnp.exp2(scores - jnp.concatenate([after] * (KEYS // HD), axis=1))
            rescale = jnp.exp2(before - after)
            acc_ref[head] = acc_ref[head] * jnp.concatenate(
                [rescale, rescale], axis=1
            ) + jnp.dot(
                probs.astype(jnp.bfloat16), values, preferred_element_type=jnp.float32
            )

    pl.loop(low, full_low)(lambda number: block(number, True))
    pl.loop(full_low, full_high)(lambda number: block(number, False))
    pl.loop(full_high, high)(lambda number: block(number, True))
    for head in range(heads):
        o_ref[:, head * HD : (head + 1) * HD] = (
            acc_ref[head, :, :HD] / acc_ref[head, :, HD:]
        ).astype(o_ref.dtype)


def attend(queries, kv, starts, query_start, kv_heads):
    rows, columns = queries.shape
    total = kv.shape[0]
    group = columns // HD // kv_heads
    tiles = rows // ROWS
    ends = jnp.stack([starts[::ROWS], starts[ROWS - 1 :: ROWS]], axis=1).reshape(-1)
    bounds = jnp.concatenate([query_start[None], ends]).astype(jnp.int32)
    return pl.pallas_call(
        attend_kernel,
        grid_spec=pltpu.PrefetchScalarGridSpec(
            num_scalar_prefetch=1,
            grid=(kv_heads, tiles),
            in_specs=[
                pl.BlockSpec((ROWS, group * HD), lambda h, t, b: (t, h)),
                pl.BlockSpec((total, HD), lambda h, t, b: (0, h)),
                pl.BlockSpec((total, HD), lambda h, t, b: (0, kv_heads + h)),
                pl.BlockSpec((ROWS, 1), lambda h, t, b: (t, 0)),
            ],
            out_specs=pl.BlockSpec((ROWS, group * HD), lambda h, t, b: (t, h)),
            scratch_shapes=[
                pltpu.VMEM((group, ROWS, HD), jnp.float32),
                pltpu.VMEM((group, ROWS, 2 * HD), jnp.float32),
            ],
        ),
        out_shape=jax.ShapeDtypeStruct((rows, columns), jnp.bfloat16),
        compiler_params=pltpu.CompilerParams(vmem_limit_bytes=VMEM_BYTES),
        cost_estimate=pl.CostEstimate(
            flops=2 * rows * columns * total,
            bytes_accessed=2 * (2 * rows * columns + 2 * total * kv_heads * HD),
            transcendentals=rows * columns // HD * total // 2,
        ),
    )(bounds, queries, kv, kv, starts[:, None])


def local(tokens, segment_ids, q_weight, k_weight, v_weight, o_weight):
    feat_count = lax.axis_size("feat")
    feat_index = lax.axis_index("feat")
    head_count = q_weight.shape[1] // HD
    group = H // KVH
    kv_width = max(KVD // feat_count, HD)
    kv_heads = kv_width // HD
    kv_start = feat_index * head_count // group * HD
    query_count = tokens.shape[0]
    query_start = lax.axis_index("seq") * query_count
    positions = query_start + jnp.arange(query_count, dtype=jnp.int32)
    cosine, sine = rope_tables(positions)
    factor = math.log2(math.e) / math.sqrt(HD)

    segments = jnp.concatenate(exchange(segment_ids, "seq")[0])
    starts = jnp.sum(
        segments[None, :] < segment_ids[:, None], axis=1, dtype=jnp.int32
    )
    kv_slice = jnp.concatenate(
        [
            lax.dynamic_slice_in_dim(k_weight, kv_start, kv_width, 1),
            lax.dynamic_slice_in_dim(v_weight, kv_start, kv_width, 1),
        ],
        axis=1,
    )
    zero = jnp.zeros((1,), jnp.int32)
    pieces, numbers = exchange(tokens, "feat")
    sources = jnp.stack([feat_index ^ number for number in numbers])
    token_rows = sources * tokens.shape[1]
    kv_panel = lax.all_gather(kv_slice, "seq", axis=0, tiled=True)
    kv_local = project(
        pieces, token_rows, [kv_panel], zero, (cosine, sine), kv_width, 1
    )
    q_pieces, q_numbers = exchange(q_weight, "seq")
    seq_index = lax.axis_index("seq")
    q_rows = jnp.stack([seq_index ^ number for number in q_numbers]) * q_weight.shape[0]
    kv = lax.all_gather(kv_local, "seq", axis=0, tiled=True)
    queries = project(
        pieces,
        token_rows,
        q_pieces,
        q_rows,
        (cosine * factor, sine * factor),
        256,
        "all",
    )
    o_panel = lax.all_gather(o_weight, "seq", axis=0, tiled=True)
    attended = attend(queries, kv, starts, query_start, kv_heads)
    mixed, _ = exchange(attended, "feat")
    attended_rows = sources * attended.shape[1]
    return project(
        mixed, attended_rows, [o_panel], zero, (cosine, sine), 256, "none"
    )


def solution(mesh):
    in_specs = (
        P("seq", "feat"),
        P("seq"),
        P("seq", "feat"),
        P("seq", None),
        P("seq", None),
        P("seq", "feat"),
    )
    out_specs = P("seq", "feat")
    return jax.shard_map(local, mesh=mesh, in_specs=in_specs, out_specs=out_specs, check_vma=False)
```

```python
import functools
import math

import jax
import jax.numpy as jnp
from jax import lax
from jax.experimental import pallas as pl
from jax.experimental.pallas import tpu as pltpu
from jax.sharding import PartitionSpec as P

H = 32
KVH = 8
HD = 128
KVD = 1024
rope_base = 500000.0
VMEM_BYTES = 48 * 1024 * 1024
ROWS = 256
KEYS = 512


def rope_tables(positions):
    lane = jnp.arange(HD, dtype=jnp.int32)
    pair_index = (lane // 2).astype(jnp.float32)
    frequency = jnp.exp(-(2.0 * pair_index / HD) * math.log(rope_base))
    angle = positions.astype(jnp.float32)[:, None] * frequency[None, :]
    sign = jnp.where(lane % 2 == 0, -1.0, 1.0)
    return jnp.cos(angle), jnp.sin(angle) * sign[None, :]


def project_kernel(rope_tiles, count, w_count, offsets, w_offsets, *refs):
    x_refs = refs[:count]
    w_refs = refs[count : count + w_count]
    cos_ref, sin_ref, o_ref = refs[count + w_count : count + w_count + 3]
    column = pl.program_id(0)
    rows, depth = x_refs[0].shape
    w_ref = w_refs[0]
    if w_count > 1:
        w_ref = refs[-1]
        part_rows = w_refs[0].shape[0]
        for number in range(w_count):
            begin = pl.multiple_of(w_offsets[number], part_rows)
            w_ref[pl.ds(begin, part_rows), :] = w_refs[number][...]

    @pl.loop(0, rows // ROWS)
    def _(step):
        at = pl.ds(pl.multiple_of(step * ROWS, ROWS), ROWS)
        raw = jnp.zeros((ROWS, w_ref.shape[1]), jnp.float32)
        for number in range(count):
            begin = pl.multiple_of(offsets[number], depth)
            raw += jnp.dot(
                x_refs[number][at, :],
                w_ref[pl.ds(begin, depth), :],
                preferred_element_type=jnp.float32,
            )

        def turned():
            cosine = cos_ref[at, :]
            sine = sin_ref[at, :]
            even = lax.broadcasted_iota(jnp.int32, (ROWS, HD), 1) % 2 == 0
            for head in range(w_ref.shape[1] // HD):
                part = raw[:, head * HD : (head + 1) * HD]
                other = jnp.where(
                    even, pltpu.roll(part, HD - 1, 1), pltpu.roll(part, 1, 1)
                )
                o_ref[at, head * HD : (head + 1) * HD] = (
                    part * cosine + other * sine
                ).astype(o_ref.dtype)

        def plain():
            o_ref[at, :] = raw.astype(o_ref.dtype)

        if rope_tiles == "all":
            turned()
        elif rope_tiles == "none":
            plain()
        else:
            pl.when(column < rope_tiles)(turned)
            pl.when(column >= rope_tiles)(plain)


def project(pieces, offsets, w_pieces, w_offsets, tables, tile, rope_tiles):
    rows, depth = pieces[0].shape
    total = depth * len(pieces)
    columns = w_pieces[0].shape[1]
    whole = lambda j, o, p: (0, 0)
    return pl.pallas_call(
        functools.partial(project_kernel, rope_tiles, len(pieces), len(w_pieces)),
        grid_spec=pltpu.PrefetchScalarGridSpec(
            num_scalar_prefetch=2,
            grid=(columns // tile,),
            in_specs=[pl.BlockSpec((rows, depth), whole)] * len(pieces)
            + [
                pl.BlockSpec((total // len(w_pieces), tile), lambda j, o, p: (0, j))
            ]
            * len(w_pieces)
            + [pl.BlockSpec((rows, HD), whole)] * 2,
            out_specs=pl.BlockSpec((rows, tile), lambda j, o, p: (0, j)),
            scratch_shapes=[pltpu.VMEM((total, tile), jnp.bfloat16)]
            if len(w_pieces) > 1
            else [],
        ),
        out_shape=jax.ShapeDtypeStruct((rows, columns), jnp.bfloat16),
        compiler_params=pltpu.CompilerParams(vmem_limit_bytes=VMEM_BYTES),
        cost_estimate=pl.CostEstimate(
            flops=2 * rows * total * columns,
            bytes_accessed=2 * (rows * total + total * columns + rows * columns),
            transcendentals=0,
        ),
    )(offsets, w_offsets, *pieces, *w_pieces, *tables)


def exchange(block, axis):
    count = lax.axis_size(axis)
    pieces, numbers = [block], [0]
    bit = count // 2
    while bit:
        pairs = [(index, index ^ bit) for index in range(count)]
        pieces = pieces + [lax.ppermute(piece, axis, pairs) for piece in pieces]
        numbers = numbers + [number ^ bit for number in numbers]
        bit //= 2
    return pieces, numbers


def attend_kernel(bounds, q_ref, k_ref, v_ref, start_ref, o_ref, m_ref, acc_ref):
    tile = pl.program_id(1)
    heads = q_ref.shape[1] // HD
    begin = bounds[0] + tile * ROWS
    first_start = bounds[1 + 2 * tile]
    last_start = bounds[2 + 2 * tile]
    low = first_start // KEYS
    high = (begin + ROWS - 1) // KEYS + 1
    full_low = jnp.minimum((last_start + KEYS - 1) // KEYS, high)
    full_high = jnp.clip((begin + 1) // KEYS, full_low, high)
    m_ref[...] = jnp.full(m_ref.shape, -1e30, jnp.float32)
    acc_ref[...] = jnp.zeros(acc_ref.shape, jnp.float32)
    ones = jnp.ones((KEYS, HD), jnp.bfloat16)

    def block(number, masked):
        at = pl.ds(pl.multiple_of(number * KEYS, KEYS), KEYS)
        keys = k_ref[at, :]
        values = jnp.concatenate([v_ref[at, :], ones], axis=1)
        if masked:
            key_at = number * KEYS + lax.broadcasted_iota(jnp.int32, (ROWS, KEYS), 1)
            query_at = begin + lax.broadcasted_iota(jnp.int32, (ROWS, KEYS), 0)
            allowed = (key_at <= query_at) & (key_at >= start_ref[...])
        for head in range(heads):
            scores = lax.dot_general(
                q_ref[:, head * HD : (head + 1) * HD],
                keys,
                (((1,), (1,)), ((), ())),
                preferred_element_type=jnp.float32,
            )
            if masked:
                scores = jnp.where(allowed, scores, -1e30)
            before = m_ref[head]
            after = jnp.maximum(before, jnp.max(scores, axis=1, keepdims=True))
            m_ref[head] = after
            probs = jnp.exp2(scores - jnp.concatenate([after] * (KEYS // HD), axis=1))
            rescale = jnp.exp2(before - after)
            acc_ref[head] = acc_ref[head] * jnp.concatenate(
                [rescale, rescale], axis=1
            ) + jnp.dot(
                probs.astype(jnp.bfloat16), values, preferred_element_type=jnp.float32
            )

    pl.loop(low, full_low)(lambda number: block(number, True))
    pl.loop(full_low, full_high)(lambda number: block(number, False))
    pl.loop(full_high, high)(lambda number: block(number, True))
    for head in range(heads):
        o_ref[:, head * HD : (head + 1) * HD] = (
            acc_ref[head, :, :HD] / acc_ref[head, :, HD:]
        ).astype(o_ref.dtype)


def attend(queries, kv, starts, query_start, kv_heads):
    rows, columns = queries.shape
    total = kv.shape[0]
    group = columns // HD // kv_heads
    tiles = rows // ROWS
    ends = jnp.stack([starts[::ROWS], starts[ROWS - 1 :: ROWS]], axis=1).reshape(-1)
    bounds = jnp.concatenate([query_start[None], ends]).astype(jnp.int32)
    return pl.pallas_call(
        attend_kernel,
        grid_spec=pltpu.PrefetchScalarGridSpec(
            num_scalar_prefetch=1,
            grid=(kv_heads, tiles),
            in_specs=[
                pl.BlockSpec((ROWS, group * HD), lambda h, t, b: (t, h)),
                pl.BlockSpec((total, HD), lambda h, t, b: (0, h)),
                pl.BlockSpec((total, HD), lambda h, t, b: (0, kv_heads + h)),
                pl.BlockSpec((ROWS, 1), lambda h, t, b: (t, 0)),
            ],
            out_specs=pl.BlockSpec((ROWS, group * HD), lambda h, t, b: (t, h)),
            scratch_shapes=[
                pltpu.VMEM((group, ROWS, HD), jnp.float32),
                pltpu.VMEM((group, ROWS, 2 * HD), jnp.float32),
            ],
        ),
        out_shape=jax.ShapeDtypeStruct((rows, columns), jnp.bfloat16),
        compiler_params=pltpu.CompilerParams(vmem_limit_bytes=VMEM_BYTES),
        cost_estimate=pl.CostEstimate(
            flops=2 * rows * columns * total,
            bytes_accessed=2 * (2 * rows * columns + 2 * total * kv_heads * HD),
            transcendentals=rows * columns // HD * total // 2,
        ),
    )(bounds, queries, kv, kv, starts[:, None])


def local(tokens, segment_ids, q_weight, k_weight, v_weight, o_weight):
    feat_count = lax.axis_size("feat")
    feat_index = lax.axis_index("feat")
    head_count = q_weight.shape[1] // HD
    group = H // KVH
    kv_width = max(KVD // feat_count, HD)
    kv_heads = kv_width // HD
    kv_start = feat_index * head_count // group * HD
    query_count = tokens.shape[0]
    query_start = lax.axis_index("seq") * query_count
    positions = query_start + jnp.arange(query_count, dtype=jnp.int32)
    cosine, sine = rope_tables(positions)
    factor = math.log2(math.e) / math.sqrt(HD)

    segments = jnp.concatenate(exchange(segment_ids, "seq")[0])
    starts = jnp.sum(
        segments[None, :] < segment_ids[:, None], axis=1, dtype=jnp.int32
    )
    kv_slice = jnp.concatenate(
        [
            lax.dynamic_slice_in_dim(k_weight, kv_start, kv_width, 1),
            lax.dynamic_slice_in_dim(v_weight, kv_start, kv_width, 1),
        ],
        axis=1,
    )
    zero = jnp.zeros((1,), jnp.int32)
    pieces, numbers = exchange(tokens, "feat")
    sources = jnp.stack([feat_index ^ number for number in numbers])
    token_rows = sources * tokens.shape[1]
    kv_panel = lax.all_gather(kv_slice, "seq", axis=0, tiled=True)
    q_pieces, q_numbers = exchange(q_weight, "seq")
    first, starts = lax.optimization_barrier((pieces[0], starts))
    kv_local = project(
        [first] + pieces[1:], token_rows, [kv_panel], zero, (cosine, sine), kv_width, 1
    )
    seq_index = lax.axis_index("seq")
    q_rows = jnp.stack([seq_index ^ number for number in q_numbers]) * q_weight.shape[0]
    kv = lax.all_gather(kv_local, "seq", axis=0, tiled=True)
    queries = project(
        pieces,
        token_rows,
        q_pieces,
        q_rows,
        (cosine * factor, sine * factor),
        256,
        "all",
    )
    o_panel = lax.all_gather(o_weight, "seq", axis=0, tiled=True)
    attended = attend(queries, kv, starts, query_start, kv_heads)
    mixed, _ = exchange(attended, "feat")
    attended_rows = sources * attended.shape[1]
    return project(
        mixed, attended_rows, [o_panel], zero, (cosine, sine), 256, "none"
    )


def solution(mesh):
    in_specs = (
        P("seq", "feat"),
        P("seq"),
        P("seq", "feat"),
        P("seq", None),
        P("seq", None),
        P("seq", "feat"),
    )
    out_specs = P("seq", "feat")
    return jax.shard_map(local, mesh=mesh, in_specs=in_specs, out_specs=out_specs, check_vma=False)
```
